32 devices in a mesh: groups: 2 (over y), dp: 4 (over x, core), mp: 4 (over z).
Axes of the slice: x: 2, y: 2, z: 4, core: 2. Of those that a mesh axis runs over, the one named last changes fastest.
Arguments:
- hidden: bfloat16 [2, 16, 4, 8192], P(None, 'groups', 'dp', 'mp'), parts along dimension 1, may hold values from -60 to 60
- gain: float32 [8192], P('mp'), may hold values from 0.1 to 1.9
- w_query: bfloat16 [8192, 4096], P('mp'), may hold values from -0.0625 to 0.0625
- w_key: bfloat16 [8192, 512], P('mp'), may hold values from -0.1875 to 0.1875
- w_value: bfloat16 [8192, 512], P('mp'), may hold values from -0.0625 to 0.0625
- query_bias: float32 [4096], replicated, may hold values from -4 to 4
- key_bias: float32 [512], replicated, may hold values from -6 to 6
- value_bias: float32 [512], replicated, may hold values from -4 to 4
- w_out: bfloat16 [4096, 8192], P(None, 'mp'), may hold values from -0.09375 to 0.09375
- prompt_keys: bfloat16 [16, 32768, 512], P('groups', ('dp', 'mp')), parts along dimension 0, may hold values from -10 to 10
- prompt_values: bfloat16 [16, 32768, 512], P('groups', ('dp', 'mp')), parts along dimension 0, may hold values from -6 to 6
- gen_keys: bfloat16 [16, 4, 32, 512], P('groups', 'dp', 'mp'), parts along dimension 0, may hold values from -10 to 10
- gen_values: bfloat16 [16, 4, 32, 512], P('groups', 'dp', 'mp'), parts along dimension 0, may hold values from -6 to 6
- parents: int32 [2, 16, 4], P(None, 'groups'), parts along dimension 1, may hold values from 0 to 3
Outputs:
- attn_out: bfloat16 [2, 16, 4, 8192], P(None, 'groups', 'dp', 'mp'), parts along dimension 1
The draws below stay inside these ranges and needn't reach their ends.
There are 2 independent parts, one for each index of `groups`. The reference program is written for one: setup_inputs(seed, part) draws one part's arguments, and reference() takes and returns one part's arrays. A program takes and returns all parts, laid end to end along the dimension named above; an argument that names none is the same for every part. Nothing has to cross between parts.
All inputs are finite; a program needn't handle non-finite values.
Results may differ from the reference program's by a relative error of at most 0.0098.
Values may be sent and summed in bfloat16 or wider, within the bound.
A program may use at most 192 MiB of HBM per device.

```python
import jax
import jax.numpy as jnp
from jax import lax

D = 8192
QH = 32
KVH = 4
HD = 128
BEAMS = 4
STEPS = 2
PROMPTS = 8
LEN = 32768
GEN = 32
QW = 4096
KVW = 512


def draw_hidden(key, part):
    column = jnp.arange(D, dtype=jnp.float32)
    ramp = jnp.exp(jnp.log(3.0) * column / D)
    entries = jnp.clip(jax.random.normal(key, (STEPS, PROMPTS, BEAMS, D), jnp.float32), -4.0, 4.0)
    drawn = entries * ramp
    return drawn.astype(jnp.bfloat16)


def draw_query_bias(key, part):
    drawn = jnp.clip(jax.random.normal(key, (QH * HD,), jnp.float32), -4.0, 4.0)
    return drawn


def draw_key_bias(key, part):
    drawn = jnp.clip(jax.random.normal(key, (KVH * HD,), jnp.float32), -4.0, 4.0)
    return drawn


def draw_prompt_keys(key, part):
    drawn = 2.0 * jnp.clip(jax.random.normal(key, (PROMPTS, LEN, KVH * HD), jnp.float32), -5.0, 5.0)
    return drawn.astype(jnp.bfloat16)


def place_ends(values, key, low, high):
    place = [jax.random.randint(jax.random.fold_in(key, axis), (), 0, length) for axis, length in enumerate(values.shape)]
    widest = values.shape.index(max(values.shape))
    next_to = place[:widest] + [(place[widest] + 1) % values.shape[widest]] + place[widest + 1:]
    return values.at[tuple(place)].set(low).at[tuple(next_to)].set(high)


def shard_levels(key, dims, split, smallest, high):
    level = 1.0
    for dim, blocks in split:
        steps = jax.random.uniform(jax.random.fold_in(jax.random.fold_in(key, 6), dim), (blocks,), jnp.float32, smallest / len(split), high / len(split))
        level = level * jnp.repeat(jnp.exp(steps), dims[dim] // blocks).reshape((-1,) + (1,) * (len(dims) - 1 - dim))
    return level


def centred(rng, extent, spread, limit, split=(), held_as=jnp.bfloat16):
    values = spread * jax.random.normal(rng, extent, jnp.float32)
    if split:
        values = values * shard_levels(rng, extent, split, -0.22, 0.18)
    return jnp.clip(values, -limit, limit).astype(held_as)


def setup_inputs(seed: int = 0, part: int = 0) -> dict:
    seeds = jax.random.split(jax.random.key(seed), 15)
    part_keys = jax.random.split(jax.random.fold_in(seeds[14], part), 15)
    hidden = draw_hidden(jax.random.fold_in(jax.random.fold_in(seeds[14], part), 71), part)
    gain = jnp.clip(1.0 + 0.18 * jax.random.normal(seeds[1], (D,), jnp.float32), 0.1, 1.9)
    w_query = centred(seeds[2], (D, QW), D ** -0.5, 0.0625, ((0, 4),))
    w_key = centred(seeds[3], (D, KVW), (D // 9) ** -0.5, 0.1875, ((0, 4),))
    w_value = centred(seeds[4], (D, KVW), D ** -0.5, 0.0625, ((0, 4),))
    query_bias = draw_query_bias(jax.random.fold_in(seeds[14], 71), part)
    key_bias = draw_key_bias(jax.random.fold_in(seeds[14], 71), part)
    value_bias = centred(seeds[7], (KVW,), 1.0, 4.0, (), jnp.float32)
    w_out = centred(seeds[8], (QW, D), QW ** -0.5, 0.09375, ((1, 4),))
    prompt_keys = draw_prompt_keys(jax.random.fold_in(jax.random.fold_in(seeds[14], part), 71), part)
    prompt_values = centred(part_keys[10], (PROMPTS, LEN, KVW), 1.0, 6.0, ((1, 16),))
    gen_keys = centred(part_keys[11], (PROMPTS, BEAMS, GEN, KVW), 2.0, 10.0, ((1, 4), (2, 4)))
    gen_values = centred(part_keys[12], (PROMPTS, BEAMS, GEN, KVW), 1.0, 6.0, ((1, 4), (2, 4)))
    parents = place_ends(jax.random.randint(part_keys[13], (STEPS, PROMPTS, BEAMS), 0, BEAMS), jax.random.fold_in(part_keys[13], 1), 0, BEAMS - 1).astype(jnp.int32)
    return {"hidden": hidden, "gain": gain, "w_query": w_query, "w_key": w_key, "w_value": w_value, "query_bias": query_bias, "key_bias": key_bias, "value_bias": value_bias, "w_out": w_out, "prompt_keys": prompt_keys, "prompt_values": prompt_values, "gen_keys": gen_keys, "gen_values": gen_values, "parents": parents}


def split_heads(array):
    return array.reshape(array.shape[:-1] + (KVH, QH // KVH, HD))

def split_kv(array):
    return array.reshape(array.shape[:-1] + (KVH, HD))

def project(hidden_step, gain, w_query, w_key, w_value, query_bias, key_bias, value_bias):
    widened = hidden_step.astype(jnp.float32)
    inverse = lax.rsqrt(lax.optimization_barrier(jnp.mean(widened * widened, axis=-1)) + 1e-06)[..., None]
    scaled = (widened * gain).astype(jnp.bfloat16).reshape(-1, D)
    results = []
    for weight, bias in ((w_query, query_bias), (w_key, key_bias), (w_value, value_bias)):
        product = jnp.dot(scaled, weight, preferred_element_type=jnp.float32)
        product = product.reshape(hidden_step.shape[:-1] + (weight.shape[1],))
        results.append((product * inverse + bias).astype(jnp.bfloat16))
    return results

def lineage(parents, step, stop):
    source = jnp.broadcast_to(jnp.arange(BEAMS, dtype=jnp.int32)[None, :], parents.shape[1:])
    for later in range(step, stop, -1):
        source = jnp.take_along_axis(parents[later], source, axis=1)
    return source

def reference(hidden, gain, w_query, w_key, w_value, query_bias, key_bias, value_bias, w_out, prompt_keys, prompt_values, gen_keys, gen_values, parents):
    factor = HD ** (-0.5)
    prompt_k = split_kv(prompt_keys).astype(jnp.float32)
    prompt_v = split_kv(prompt_values).astype(jnp.float32)
    fresh_keys = []
    fresh_values = []
    outputs = []
    for step in range(STEPS):
        query, new_key, new_value = project(hidden[step], gain, w_query, w_key, w_value, query_bias, key_bias, value_bias)
        anchor = lineage(parents, step, -1)
        extra_keys = [jnp.take_along_axis(gen_keys, anchor[:, :, None, None], axis=1)]
        extra_values = [jnp.take_along_axis(gen_values, anchor[:, :, None, None], axis=1)]
        for earlier in range(step):
            source = lineage(parents, step, earlier)
            extra_keys.append(jnp.take_along_axis(fresh_keys[earlier], source[:, :, None], axis=1)[:, :, None])
            extra_values.append(jnp.take_along_axis(fresh_values[earlier], source[:, :, None], axis=1)[:, :, None])
        extra_keys.append(new_key[:, :, None])
        extra_values.append(new_value[:, :, None])
        keys_extra = split_kv(jnp.concatenate(extra_keys, axis=2)).astype(jnp.float32)
        values_extra = split_kv(jnp.concatenate(extra_values, axis=2)).astype(jnp.float32)
        grouped = split_heads(query).astype(jnp.float32)
        prompt_scores = jnp.einsum('pbgrd,plgd->pbgrl', grouped, prompt_k) * factor
        extra_scores = jnp.einsum('pbgrd,pbngd->pbgrn', grouped, keys_extra) * factor
        top = jnp.maximum(lax.optimization_barrier(jnp.max(prompt_scores, axis=-1)), lax.optimization_barrier(jnp.max(extra_scores, axis=-1)))
        prompt_weights = jnp.exp(prompt_scores - top[..., None]).astype(jnp.bfloat16)
        extra_weights = jnp.exp(extra_scores - top[..., None]).astype(jnp.bfloat16)
        total = lax.optimization_barrier(jnp.sum(prompt_weights.astype(jnp.float32), axis=-1)) + lax.optimization_barrier(jnp.sum(extra_weights.astype(jnp.float32), axis=-1))
        numerator = jnp.einsum('pbgrl,plgd->pbgrd', prompt_weights.astype(jnp.float32), prompt_v)
        numerator = numerator + jnp.einsum('pbgrn,pbngd->pbgrd', extra_weights.astype(jnp.float32), values_extra)
        attended = (numerator / total[..., None]).reshape(PROMPTS * BEAMS, QW).astype(jnp.bfloat16)
        result = jnp.dot(attended, w_out, preferred_element_type=jnp.float32)
        outputs.append(result.reshape(PROMPTS, BEAMS, D).astype(jnp.bfloat16))
        fresh_keys.append(new_key)
        fresh_values.append(new_value)
    return jnp.stack(outputs)
```

```python
import functools

import jax
import jax.numpy as jnp
from jax import lax
from jax.experimental import pallas as pl
from jax.experimental.pallas import tpu as pltpu
from jax.sharding import PartitionSpec as P

D = 8192
QH = 32
KVH = 4
HD = 128
REPEAT = QH // KVH
HEADS = QH + 2 * KVH
MESH = pl.DeviceIdType.MESH
VMEM_LIMIT = 48 * 1024 * 1024
hidden_fill = -1e30


def exchange_kernel(
    dp_count,
    mp_count,
    per_rank,
    query_ref,
    key_ref,
    value_ref,
    squares_ref,
    bias_ref,
    out_ref,
    parts,
    landed,
    gathered,
    reduce_send,
    reduce_recv,
    spread_send,
    spread_recv,
    far_send,
    far_recv,
    near_send,
    near_recv,
):
    beam = lax.axis_index("dp")
    rank = lax.axis_index("mp")
    rows = squares_ref.shape[0]
    far = lax.rem(beam + dp_count // 2, dp_count)
    near = beam + 1 - 2 * lax.rem(beam, 2)

    barrier = pltpu.get_barrier_semaphore()
    for delta in range(1, mp_count):
        pl.semaphore_signal(
            barrier,
            inc=1,
            device_id={"mp": lax.rem(rank + delta, mp_count)},
            device_id_type=MESH,
        )
    for partner in (far, near):
        pl.semaphore_signal(barrier, inc=1, device_id={"dp": partner}, device_id_type=MESH)

    for owner in range(mp_count):
        for place in range(per_rank):
            head = owner * per_rank + place
            if head < QH:
                part = query_ref[:, head * HD : (head + 1) * HD]
            elif head < QH + KVH:
                part = key_ref[:, (head - QH) * HD : (head - QH + 1) * HD]
            elif head < HEADS:
                first = (head - QH - KVH) * HD
                part = value_ref[:, first : first + HD]
            else:
                part = jnp.zeros((rows, HD), jnp.float32)
            parts[owner, place] = part
        parts[owner, per_rank] = squares_ref[...]
    pl.semaphore_wait(barrier, mp_count + 1)

    def reduce_copy(delta):
        peer = lax.rem(rank + delta, mp_count)
        return pltpu.make_async_remote_copy(
            src_ref=parts.at[peer],
            dst_ref=landed.at[delta],
            send_sem=reduce_send.at[delta],
            recv_sem=reduce_recv.at[delta],
            device_id={"mp": peer},
            device_id_type=MESH,
        )

    for delta in range(1, mp_count):
        reduce_copy(delta).start()
    total = parts[rank]
    for delta in range(1, mp_count):
        reduce_copy(delta).wait_recv()
        total = total + landed[delta]
    inverse = lax.rsqrt(total[per_rank] / D + 1e-06)
    mine = pl.ds(rank * per_rank, per_rank)
    done = total[:per_rank] * inverse[None] + bias_ref[mine][:, None, :]
    gathered[beam, mine] = done.astype(jnp.bfloat16)

    def spread_copy(delta):
        peer = lax.rem(rank + delta, mp_count)
        return pltpu.make_async_remote_copy(
            src_ref=gathered.at[beam, mine],
            dst_ref=gathered.at[beam, mine],
            send_sem=spread_send.at[delta],
            recv_sem=spread_recv.at[delta],
            device_id={"mp": peer},
            device_id_type=MESH,
        )

    def dp_copy(delta, source_beam, partner, send, recv, slot):
        owner = lax.rem(rank - delta + mp_count, mp_count)
        block = pl.ds(owner * per_rank, per_rank)
        return pltpu.make_async_remote_copy(
            src_ref=gathered.at[source_beam, block],
            dst_ref=gathered.at[source_beam, block],
            send_sem=send.at[slot, delta],
            recv_sem=recv.at[slot, delta],
            device_id={"dp": partner},
            device_id_type=MESH,
        )

    for delta in range(1, mp_count):
        spread_copy(delta).start()
    for delta in range(mp_count):
        if delta:
            spread_copy(delta).wait_recv()
        dp_copy(delta, beam, far, far_send, far_recv, 0).start()
        dp_copy(delta, beam, near, near_send, near_recv, 0).start()
    for delta in range(mp_count):
        dp_copy(delta, beam, far, far_send, far_recv, 0).wait_recv()
        dp_copy(delta, far, near, near_send, near_recv, 1).start()
    for delta in range(mp_count):
        dp_copy(delta, beam, near, near_send, near_recv, 0).wait_recv()
        dp_copy(delta, far, near, near_send, near_recv, 1).wait_recv()
    for delta in range(mp_count):
        if delta:
            reduce_copy(delta).wait_send()
            spread_copy(delta).wait_send()
        dp_copy(delta, beam, far, far_send, far_recv, 0).wait_send()
        dp_copy(delta, beam, near, near_send, near_recv, 0).wait_send()
        dp_copy(delta, far, near, near_send, near_recv, 1).wait_send()
    out_ref[...] = gathered[...]


def exchange(query, key, value, squares, bias, dp_count, mp_count, per_rank):
    rows = squares.shape[0]
    heads = mp_count * per_rank
    vmem = pl.BlockSpec(memory_space=pltpu.VMEM)
    dma = pltpu.SemaphoreType.DMA
    return pl.pallas_call(
        functools.partial(exchange_kernel, dp_count, mp_count, per_rank),
        out_shape=jax.ShapeDtypeStruct((dp_count, heads, rows, HD), jnp.bfloat16),
        in_specs=[vmem] * 5,
        out_specs=vmem,
        scratch_shapes=[
            pltpu.VMEM((mp_count, per_rank + 1, rows, HD), jnp.float32),
            pltpu.VMEM((mp_count, per_rank + 1, rows, HD), jnp.float32),
            pltpu.VMEM((dp_count, heads, rows, HD), jnp.bfloat16),
            dma((mp_count,)),
            dma((mp_count,)),
            dma((mp_count,)),
            dma((mp_count,)),
            dma((1, mp_count)),
            dma((1, mp_count)),
            dma((2, mp_count)),
            dma((2, mp_count)),
        ],
        compiler_params=pltpu.CompilerParams(
            collective_id=0, has_side_effects=True, vmem_limit_bytes=VMEM_LIMIT
        ),
        name="exchange",
    )(query, key, value, squares, bias)


def attend_kernel(
    query_ref, key_ref, value_ref, extra_key_ref, extra_value_ref, mask_ref, out_ref, stat_ref
):
    pair = pl.program_id(1)
    factor = HD ** (-0.5)
    contract_last = (((1,), (1,)), ((), ()))
    query = query_ref[0, 0]
    rows = query.shape[0]
    scores = lax.dot_general(
        query, key_ref[0], contract_last, preferred_element_type=jnp.float32
    )
    extra = lax.dot_general(
        query, extra_key_ref[0], contract_last, preferred_element_type=jnp.float32
    )
    extra = extra + mask_ref[0]
    top = jnp.maximum(
        jnp.max(scores, axis=-1, keepdims=True), jnp.max(extra, axis=-1, keepdims=True)
    )
    weights = jnp.exp((scores - top) * factor)
    extra_weights = jnp.exp((extra - top) * factor)
    total = jnp.sum(weights, axis=-1, keepdims=True) + jnp.sum(
        extra_weights, axis=-1, keepdims=True
    )
    numerator = jnp.dot(
        weights.astype(jnp.bfloat16), value_ref[0], preferred_element_type=jnp.float32
    ) + jnp.dot(
        extra_weights.astype(jnp.bfloat16), extra_value_ref[0], preferred_element_type=jnp.float32
    )
    row = lax.broadcasted_iota(jnp.int32, (rows, HD), 0)
    second = lax.rem(row // (rows // 8), 2) == 1
    own = jnp.where(second, numerator[:, HD:], numerator[:, :HD])
    out_ref[0, 0] = (own / total).astype(jnp.bfloat16)
    level = top * factor + jnp.log(total)
    flat = jnp.transpose(jnp.broadcast_to(level, (rows, HD)))
    stat_ref[0, pl.ds(pair, 1), :] = flat[:1]


def attend(query, prompt_keys, prompt_values, extra_keys, extra_values, mask):
    prompts, pairs, rows, wide = query.shape
    length = prompt_keys.shape[1]
    extras = extra_keys.shape[1]
    return pl.pallas_call(
        attend_kernel,
        grid=(prompts, pairs),
        out_shape=(
            jax.ShapeDtypeStruct((prompts, pairs, rows, HD), jnp.bfloat16),
            jax.ShapeDtypeStruct((prompts, 8, rows), jnp.float32),
        ),
        in_specs=[
            pl.BlockSpec((1, 1, rows, wide), lambda p, h: (p, h, 0, 0)),
            pl.BlockSpec((1, length, wide), lambda p, h: (p, 0, h)),
            pl.BlockSpec((1, length, wide), lambda p, h: (p, 0, h)),
            pl.BlockSpec((1, extras, wide), lambda p, h: (p, 0, h)),
            pl.BlockSpec((1, extras, wide), lambda p, h: (p, 0, h)),
            pl.BlockSpec((1, rows, extras), lambda p, h: (p, 0, 0)),
        ],
        out_specs=(
            pl.BlockSpec((1, 1, rows, HD), lambda p, h: (p, h, 0, 0)),
            pl.BlockSpec((1, 8, rows), lambda p, h: (p, 0, 0)),
        ),
        compiler_params=pltpu.CompilerParams(vmem_limit_bytes=VMEM_LIMIT),
        name="attend",
    )(query, prompt_keys, prompt_values, extra_keys, extra_values, mask)


def region(rank, prompts, mp_count):
    if mp_count <= prompts:
        each = prompts // mp_count
        return rank * each, each, 0, 2, 0, 32
    share = mp_count // prompts
    place = lax.rem(rank, share)
    if share == 2:
        return rank // share, 1, place, 1, 0, 32
    return rank // share, 1, place // 2, 1, lax.rem(place, 2) * 16, 16


def combine_kernel(
    dp_count,
    mp_count,
    out_in,
    stat_in,
    out_ref,
    outs,
    stats,
    landed,
    landed_stats,
    flipped,
    gathered,
    out_send,
    out_recv,
    stat_send,
    stat_recv,
    spread_send,
    spread_recv,
):
    beam = lax.axis_index("dp")
    rank = lax.axis_index("mp")
    count = dp_count * mp_count
    me = beam * mp_count + rank
    prompts = out_in.shape[0]
    beam_rows = out_in.shape[2] // dp_count

    barrier = pltpu.get_barrier_semaphore()

    def greet(delta, carry):
        peer = lax.rem(me + delta, count)
        pl.semaphore_signal(
            barrier,
            inc=1,
            device_id={"dp": peer // mp_count, "mp": lax.rem(peer, mp_count)},
            device_id_type=MESH,
        )
        return carry

    lax.fori_loop(1, count, greet, 0)
    outs[...] = out_in[...]
    stats[...] = stat_in[...]
    pl.semaphore_wait(barrier, count - 1)

    def views(peer):
        first, each, pair, pairs, row, rows = region(lax.rem(peer, mp_count), prompts, mp_count)
        start = pl.multiple_of((peer // mp_count) * beam_rows + row, 16)
        return (
            outs.at[pl.ds(first, each), pl.ds(pair, pairs), pl.ds(start, rows)],
            stats.at[pl.ds(first, each)],
        )

    def copies(delta):
        peer = lax.rem(me + delta, count)
        target = {"dp": peer // mp_count, "mp": lax.rem(peer, mp_count)}
        out_view, stat_view = views(peer)
        return (
            pltpu.make_async_remote_copy(
                src_ref=out_view,
                dst_ref=landed.at[delta],
                send_sem=out_send.at[delta],
                recv_sem=out_recv.at[delta],
                device_id=target,
                device_id_type=MESH,
            ),
            pltpu.make_async_remote_copy(
                src_ref=stat_view,
                dst_ref=landed_stats.at[delta],
                send_sem=stat_send.at[delta],
                recv_sem=stat_recv.at[delta],
                device_id=target,
                device_id_type=MESH,
            ),
        )

    def begin(delta, carry):
        for copy in copies(delta):
            copy.start()
        return carry

    def finish(delta, carry):
        for copy in copies(delta):
            copy.wait()
        return carry

    lax.fori_loop(1, count, begin, 0)
    first, each, pair, pairs, row, rows = region(rank, prompts, mp_count)
    start = pl.multiple_of(beam * beam_rows + row, 16)
    landed[0] = outs[pl.ds(first, each), pl.ds(pair, pairs), pl.ds(start, rows)]
    landed_stats[0] = stats[pl.ds(first, each)]
    lax.fori_loop(1, count, finish, 0)

    for item in range(each):
        levels = landed_stats[:, item]
        top = jnp.max(levels, axis=0, keepdims=True)
        shares = jnp.exp(levels - top)
        shares = shares / jnp.sum(shares, axis=0, keepdims=True)
        flipped[...] = jnp.transpose(shares.reshape(count * 8, shares.shape[-1]))
        columns = flipped[pl.ds(start, rows), :]
        for place in range(pairs):
            total = jnp.zeros((rows, HD), jnp.float32)
            for source in range(count):
                if pairs == 2:
                    column = columns[:, source * 8 + place : source * 8 + place + 1]
                else:
                    column = jnp.where(
                        pair == 1,
                        columns[:, source * 8 + 1 : source * 8 + 2],
                        columns[:, source * 8 : source * 8 + 1],
                    )
                total = total + column * landed[source, item, place].astype(jnp.float32)
            gathered[first + item, pair + place, pl.ds(pl.multiple_of(row, 16), rows)] = (
                total.astype(jnp.bfloat16)
            )

    def spread(delta):
        peer = lax.rem(rank + delta, mp_count)
        view = gathered.at[
            pl.ds(first, each), pl.ds(pair, pairs), pl.ds(pl.multiple_of(row, 16), rows)
        ]
        return pltpu.make_async_remote_copy(
            src_ref=view,
            dst_ref=view,
            send_sem=spread_send.at[delta],
            recv_sem=spread_recv.at[delta],
            device_id={"mp": peer},
            device_id_type=MESH,
        )

    for delta in range(1, mp_count):
        spread(delta).start()
    for delta in range(1, mp_count):
        spread(delta).wait()
    out_ref[...] = gathered[...]


def combine(outs, stats, dp_count, mp_count):
    prompts, pairs, rows, _ = outs.shape
    count = dp_count * mp_count
    _, each, _, some_pairs, _, some_rows = region(0, prompts, mp_count)
    vmem = pl.BlockSpec(memory_space=pltpu.VMEM)
    dma = pltpu.SemaphoreType.DMA
    return pl.pallas_call(
        functools.partial(combine_kernel, dp_count, mp_count),
        out_shape=jax.ShapeDtypeStruct((prompts, pairs, rows // dp_count, HD), jnp.bfloat16),
        in_specs=[vmem] * 2,
        out_specs=vmem,
        scratch_shapes=[
            pltpu.VMEM(outs.shape, jnp.bfloat16),
            pltpu.VMEM(stats.shape, jnp.float32),
            pltpu.VMEM((count, each, some_pairs, some_rows, HD), jnp.bfloat16),
            pltpu.VMEM((count, each, 8, rows), jnp.float32),
            pltpu.VMEM((rows, count * 8), jnp.float32),
            pltpu.VMEM((prompts, pairs, rows // dp_count, HD), jnp.bfloat16),
            dma((count,)),
            dma((count,)),
            dma((count,)),
            dma((count,)),
            dma((mp_count,)),
            dma((mp_count,)),
        ],
        compiler_params=pltpu.CompilerParams(
            collective_id=1, has_side_effects=True, vmem_limit_bytes=VMEM_LIMIT
        ),
        name="combine",
    )(outs, stats)


def lineage(parents, step, stop):
    beams = parents.shape[2]
    source = jnp.broadcast_to(jnp.arange(beams, dtype=jnp.int32)[None, :], parents.shape[1:])
    for later in range(step, stop, -1):
        choice = source[:, :, None] == jnp.arange(beams, dtype=jnp.int32)
        source = jnp.sum(jnp.where(choice, parents[later][:, None, :], 0), axis=-1)
    return source


def on_device(
    hidden,
    gain,
    w_query,
    w_key,
    w_value,
    query_bias,
    key_bias,
    value_bias,
    w_out,
    prompt_keys,
    prompt_values,
    gen_keys,
    gen_values,
    parents,
):
    beam = lax.axis_index("dp")
    rank = lax.axis_index("mp")
    beams = lax.axis_size("dp")
    mp_count = lax.axis_size("mp")
    steps, prompts = hidden.shape[:2]
    rows = steps * prompts
    per_rank = -(-HEADS // mp_count)

    widened = hidden.reshape(rows, -1).astype(jnp.float32)
    squares = jnp.sum(widened * widened, axis=-1, keepdims=True)
    scaled = (widened * gain).astype(jnp.bfloat16)
    partial = [
        jnp.dot(scaled, weight, preferred_element_type=jnp.float32)
        for weight in (w_query, w_key, w_value)
    ]
    bias = jnp.concatenate([query_bias, key_bias, value_bias]).reshape(HEADS, HD)
    bias = jnp.pad(bias, ((0, per_rank * mp_count - HEADS), (0, 0)))
    projected = exchange(
        *partial, jnp.broadcast_to(squares, (rows, HD)), bias, beams, mp_count, per_rank
    )

    query = projected[:, :QH].reshape(beams, 2, 2, REPEAT, steps, prompts, HD)
    query = query.transpose(5, 1, 0, 2, 4, 3, 6)
    split = jnp.arange(2)
    same = (split[:, None] == split[None, :])[None, None, None, :, None, None, :, None]
    query = jnp.where(same, query[:, :, :, :, :, :, None, :], jnp.bfloat16(0))
    query = query.reshape(prompts, 2, beams * 2 * steps * REPEAT, 2 * HD)

    own = lax.dynamic_index_in_dim(projected, beam, 0, keepdims=False)
    fresh = own[QH:HEADS].reshape(2, KVH, steps, prompts, HD).transpose(0, 3, 2, 1, 4)
    fresh = fresh.reshape(2, prompts, steps, KVH * HD)
    width = gen_keys.shape[2]
    extras = -(-(width + steps) // 16) * 16
    pad = jnp.zeros((prompts, extras - width - steps, KVH * HD), jnp.bfloat16)
    extra_keys = jnp.concatenate([gen_keys[:, 0], fresh[0], pad], axis=1)
    extra_values = jnp.concatenate([gen_values[:, 0], fresh[1], pad], axis=1)

    seen = []
    for step in range(steps):
        anchor = lineage(parents, step, -1) == beam
        columns = [jnp.broadcast_to(anchor[:, :, None], (prompts, beams, width))]
        for source in range(steps):
            if source <= step:
                flag = (lineage(parents, step, source) == beam) & (rank == 0)
            else:
                flag = jnp.zeros((prompts, beams), jnp.bool_)
            columns.append(flag[:, :, None])
        columns.append(jnp.zeros((prompts, beams, extras - width - steps), jnp.bool_))
        seen.append(jnp.concatenate(columns, axis=2))
    mask = jnp.where(jnp.stack(seen, axis=2), jnp.float32(0), jnp.float32(hidden_fill))
    mask = jnp.broadcast_to(
        mask[:, :, None, :, None, :], (prompts, beams, 2, steps, REPEAT, extras)
    ).reshape(prompts, beams * 2 * steps * REPEAT, extras)

    outs, stats = attend(query, prompt_keys, prompt_values, extra_keys, extra_values, mask)
    attended = combine(outs, stats, beams, mp_count)
    attended = attended.reshape(prompts, 2, 2, steps, REPEAT, HD).transpose(3, 0, 1, 2, 4, 5)
    attended = attended.reshape(rows, QH * HD)
    result = jnp.dot(attended, w_out, preferred_element_type=jnp.float32).astype(jnp.bfloat16)
    return result.reshape(steps, prompts, 1, -1)


def solution(mesh):
    return jax.shard_map(
        on_device,
        mesh=mesh,
        in_specs=(
            P(None, "groups", "dp", "mp"),
            P("mp"),
            P("mp", None),
            P("mp", None),
            P("mp", None),
            P(),
            P(),
            P(),
            P(None, "mp"),
            P("groups", ("dp", "mp"), None),
            P("groups", ("dp", "mp"), None),
            P("groups", "dp", "mp", None),
            P("groups", "dp", "mp", None),
            P(None, "groups", None),
        ),
        out_specs=P(None, "groups", "dp", "mp"),
        check_vma=False,
    )
```

```python
import functools

import jax
import jax.numpy as jnp
from jax import lax
from jax.experimental import pallas as pl
from jax.experimental.pallas import tpu as pltpu
from jax.sharding import PartitionSpec as P

D = 8192
QH = 32
KVH = 4
HD = 128
REPEAT = QH // KVH
HEADS = QH + 2 * KVH
MESH = pl.DeviceIdType.MESH
VMEM_LIMIT = 48 * 1024 * 1024
hidden_fill = -1e30


def exchange_kernel(
    dp_count,
    mp_count,
    per_rank,
    query_ref,
    key_ref,
    value_ref,
    squares_ref,
    bias_ref,
    out_ref,
    parts,
    landed,
    gathered,
    reduce_send,
    reduce_recv,
    spread_send,
    spread_recv,
    far_send,
    far_recv,
    near_send,
    near_recv,
):
    beam = lax.axis_index("dp")
    rank = lax.axis_index("mp")
    rows = squares_ref.shape[0]
    far = lax.rem(beam + dp_count // 2, dp_count)
    near = beam + 1 - 2 * lax.rem(beam, 2)

    barrier = pltpu.get_barrier_semaphore()
    for delta in range(1, mp_count):
        pl.semaphore_signal(
            barrier,
            inc=1,
            device_id={"mp": lax.rem(rank + delta, mp_count)},
            device_id_type=MESH,
        )
    for partner in (far, near):
        pl.semaphore_signal(barrier, inc=1, device_id={"dp": partner}, device_id_type=MESH)

    for owner in range(mp_count):
        for place in range(per_rank):
            head = owner * per_rank + place
            if head < QH:
                part = query_ref[:, head * HD : (head + 1) * HD]
            elif head < QH + KVH:
                part = key_ref[:, (head - QH) * HD : (head - QH + 1) * HD]
            elif head < HEADS:
                first = (head - QH - KVH) * HD
                part = value_ref[:, first : first + HD]
            else:
                part = jnp.zeros((rows, HD), jnp.float32)
            parts[owner, place] = part
        parts[owner, per_rank] = squares_ref[...]
    pl.semaphore_wait(barrier, mp_count + 1)

    def reduce_copy(delta):
        peer = lax.rem(rank + delta, mp_count)
        return pltpu.make_async_remote_copy(
            src_ref=parts.at[peer],
            dst_ref=landed.at[delta],
            send_sem=reduce_send.at[delta],
            recv_sem=reduce_recv.at[delta],
            device_id={"mp": peer},
            device_id_type=MESH,
        )

    for delta in range(1, mp_count):
        reduce_copy(delta).start()
    total = parts[rank]
    for delta in range(1, mp_count):
        reduce_copy(delta).wait_recv()
        total = total + landed[delta]
    inverse = lax.rsqrt(total[per_rank] / D + 1e-06)
    mine = pl.ds(rank * per_rank, per_rank)
    done = total[:per_rank] * inverse[None] + bias_ref[mine][:, None, :]
    gathered[beam, mine] = done.astype(jnp.bfloat16)

    def spread_copy(delta):
        peer = lax.rem(rank + delta, mp_count)
        return pltpu.make_async_remote_copy(
            src_ref=gathered.at[beam, mine],
            dst_ref=gathered.at[beam, mine],
            send_sem=spread_send.at[delta],
            recv_sem=spread_recv.at[delta],
            device_id={"mp": peer},
            device_id_type=MESH,
        )

    def dp_copy(delta, source_beam, partner, send, recv, slot):
        owner = lax.rem(rank - delta + mp_count, mp_count)
        block = pl.ds(owner * per_rank, per_rank)
        return pltpu.make_async_remote_copy(
            src_ref=gathered.at[source_beam, block],
            dst_ref=gathered.at[source_beam, block],
            send_sem=send.at[slot, delta],
            recv_sem=recv.at[slot, delta],
            device_id={"dp": partner},
            device_id_type=MESH,
        )

    for delta in range(1, mp_count):
        spread_copy(delta).start()
    for delta in range(mp_count):
        if delta:
            spread_copy(delta).wait_recv()
        dp_copy(delta, beam, far, far_send, far_recv, 0).start()
        dp_copy(delta, beam, near, near_send, near_recv, 0).start()
    for delta in range(mp_count):
        dp_copy(delta, beam, far, far_send, far_recv, 0).wait_recv()
        dp_copy(delta, far, near, near_send, near_recv, 1).start()
    for delta in range(mp_count):
        dp_copy(delta, beam, near, near_send, near_recv, 0).wait_recv()
        dp_copy(delta, far, near, near_send, near_recv, 1).wait_recv()
    for delta in range(mp_count):
        if delta:
            reduce_copy(delta).wait_send()
            spread_copy(delta).wait_send()
        dp_copy(delta, beam, far, far_send, far_recv, 0).wait_send()
        dp_copy(delta, beam, near, near_send, near_recv, 0).wait_send()
        dp_copy(delta, far, near, near_send, near_recv, 1).wait_send()
    out_ref[...] = gathered[...]


def exchange(query, key, value, squares, bias, dp_count, mp_count, per_rank):
    rows = squares.shape[0]
    heads = mp_count * per_rank
    vmem = pl.BlockSpec(memory_space=pltpu.VMEM)
    dma = pltpu.SemaphoreType.DMA
    return pl.pallas_call(
        functools.partial(exchange_kernel, dp_count, mp_count, per_rank),
        out_shape=jax.ShapeDtypeStruct((dp_count, heads, rows, HD), jnp.bfloat16),
        in_specs=[vmem] * 5,
        out_specs=vmem,
        scratch_shapes=[
            pltpu.VMEM((mp_count, per_rank + 1, rows, HD), jnp.float32),
            pltpu.VMEM((mp_count, per_rank + 1, rows, HD), jnp.float32),
            pltpu.VMEM((dp_count, heads, rows, HD), jnp.bfloat16),
            dma((mp_count,)),
            dma((mp_count,)),
            dma((mp_count,)),
            dma((mp_count,)),
            dma((1, mp_count)),
            dma((1, mp_count)),
            dma((2, mp_count)),
            dma((2, mp_count)),
        ],
        compiler_params=pltpu.CompilerParams(
            collective_id=0, has_side_effects=True, vmem_limit_bytes=VMEM_LIMIT
        ),
        name="exchange",
    )(query, key, value, squares, bias)


def region(rank, prompts, mp_count):
    if mp_count <= prompts:
        each = prompts // mp_count
        return rank * each, each, 0, 2, 0, 32
    share = mp_count // prompts
    place = lax.rem(rank, share)
    if share == 2:
        return rank // share, 1, place, 1, 0, 32
    return rank // share, 1, place // 2, 1, lax.rem(place, 2) * 16, 16


def attend_kernel(
    dp_count,
    mp_count,
    query_ref,
    key_hbm,
    value_hbm,
    extra_key_ref,
    extra_value_ref,
    mask_ref,
    out_ref,
    keys,
    values,
    outs,
    stats,
    landed,
    landed_stats,
    flipped,
    gathered,
    key_sem,
    value_sem,
    out_send,
    out_recv,
    stat_send,
    stat_recv,
    spread_send,
    spread_recv,
):
    beam = lax.axis_index("dp")
    rank = lax.axis_index("mp")
    count = dp_count * mp_count
    me = beam * mp_count + rank
    prompts, pairs_all, wide_rows, wide = query_ref.shape
    beam_rows = wide_rows // dp_count
    share = max(1, mp_count // prompts)
    each = max(1, prompts // mp_count)
    factor = HD ** (-0.5)
    contract_last = (((1,), (1,)), ((), ()))
    origin = rank * each // share + each

    def place_of(turn):
        return lax.rem(origin + turn, prompts)

    def loads(turn):
        prompt = place_of(turn)
        slot = lax.rem(turn, 2)
        return (
            pltpu.make_async_copy(key_hbm.at[prompt], keys.at[slot], key_sem.at[slot]),
            pltpu.make_async_copy(value_hbm.at[prompt], values.at[slot], value_sem.at[slot]),
        )

    for copy in loads(0):
        copy.start()

    barrier = pltpu.get_barrier_semaphore()

    def greet(delta, carry):
        peer = lax.rem(me + delta, count)
        pl.semaphore_signal(
            barrier,
            inc=1,
            device_id={"dp": peer // mp_count, "mp": lax.rem(peer, mp_count)},
            device_id_type=MESH,
        )
        return carry

    lax.fori_loop(1, count, greet, 0)
    stats[...] = jnp.zeros_like(stats)
    pl.semaphore_wait(barrier, count - 1)

    def owner_of(turn, target):
        prompt = place_of(turn)
        if share > 1:
            return prompt * share + lax.rem(target, share)
        return prompt // each

    def sends(turn, target):
        prompt = place_of(turn)
        owner = owner_of(turn, target)
        other = target // share
        _, _, pair, pairs, row, rows = region(owner, prompts, mp_count)
        item = lax.rem(prompt, each)
        start = pl.multiple_of(other * beam_rows + row, 16)
        where = {"dp": other, "mp": owner}
        return (
            pltpu.make_async_remote_copy(
                src_ref=outs.at[prompt, pl.ds(pair, pairs), pl.ds(start, rows)],
                dst_ref=landed.at[me, item],
                send_sem=out_send.at[turn, target],
                recv_sem=out_recv.at[me, item],
                device_id=where,
                device_id_type=MESH,
            ),
            pltpu.make_async_remote_copy(
                src_ref=stats.at[prompt],
                dst_ref=landed_stats.at[me, item],
                send_sem=stat_send.at[turn, target],
                recv_sem=stat_recv.at[me, item],
                device_id=where,
                device_id_type=MESH,
            ),
        )

    def away(turn, target):
        return (target // share) * mp_count + owner_of(turn, target) != me

    row_id = lax.broadcasted_iota(jnp.int32, (wide_rows, HD), 0)
    second = lax.rem(row_id // (wide_rows // 8), 2) == 1

    def work(turn, carry):
        prompt = place_of(turn)
        slot = lax.rem(turn, 2)

        @pl.when(turn + 1 < prompts)
        def _():
            for copy in loads(turn + 1):
                copy.start()

        for copy in loads(turn):
            copy.wait()
        for pair in range(pairs_all):
            lanes = slice(pair * wide, (pair + 1) * wide)
            query = query_ref[prompt, pair]
            scores = lax.dot_general(
                query, keys[slot, :, lanes], contract_last, preferred_element_type=jnp.float32
            )
            extra = lax.dot_general(
                query,
                extra_key_ref[prompt, :, lanes],
                contract_last,
                preferred_element_type=jnp.float32,
            )
            extra = extra + mask_ref[prompt]
            top = jnp.maximum(
                jnp.max(scores, axis=-1, keepdims=True), jnp.max(extra, axis=-1, keepdims=True)
            )
            weights = jnp.exp((scores - top) * factor)
            extra_weights = jnp.exp((extra - top) * factor)
            total = jnp.sum(weights, axis=-1, keepdims=True) + jnp.sum(
                extra_weights, axis=-1, keepdims=True
            )
            numerator = jnp.dot(
                weights.astype(jnp.bfloat16),
                values[slot, :, lanes],
                preferred_element_type=jnp.float32,
            ) + jnp.dot(
                extra_weights.astype(jnp.bfloat16),
                extra_value_ref[prompt, :, lanes],
                preferred_element_type=jnp.float32,
            )
            own = jnp.where(second, numerator[:, HD:], numerator[:, :HD])
            outs[prompt, pair] = (own / total).astype(jnp.bfloat16)
            level = top * factor + jnp.log(total)
            flat = jnp.transpose(jnp.broadcast_to(level, (wide_rows, HD)))
            stats[prompt, pair : pair + 1] = flat[:1]
        for target in range(dp_count * share):

            @pl.when(away(turn, target))
            def _():
                for copy in sends(turn, target):
                    copy.start()

        return carry

    lax.fori_loop(0, prompts, work, 0)

    first, _, pair, pairs, row, rows = region(rank, prompts, mp_count)
    start = pl.multiple_of(beam * beam_rows + row, 16)
    landed[me] = outs[pl.ds(first, each), pl.ds(pair, pairs), pl.ds(start, rows)]
    landed_stats[me] = stats[pl.ds(first, each)]

    def finish(delta, carry):
        peer = lax.rem(me + delta, count)
        for item in range(each):
            pltpu.make_async_remote_copy(
                src_ref=landed.at[me, item],
                dst_ref=landed.at[peer, item],
                send_sem=out_send.at[0, 0],
                recv_sem=out_recv.at[peer, item],
                device_id={"dp": peer // mp_count, "mp": lax.rem(peer, mp_count)},
                device_id_type=MESH,
            ).wait_recv()
            pltpu.make_async_remote_copy(
                src_ref=landed_stats.at[me, item],
                dst_ref=landed_stats.at[peer, item],
                send_sem=stat_send.at[0, 0],
                recv_sem=stat_recv.at[peer, item],
                device_id={"dp": peer // mp_count, "mp": lax.rem(peer, mp_count)},
                device_id_type=MESH,
            ).wait_recv()
        return carry

    lax.fori_loop(1, count, finish, 0)

    for item in range(each):
        levels = landed_stats[:, item]
        top = jnp.max(levels, axis=0, keepdims=True)
        shares = jnp.exp(levels - top)
        shares = shares / jnp.sum(shares, axis=0, keepdims=True)
        flipped[...] = jnp.transpose(shares.reshape(count * 8, shares.shape[-1]))
        columns = flipped[pl.ds(start, rows), :]
        for place in range(pairs):
            total = jnp.zeros((rows, HD), jnp.float32)
            for source in range(count):
                if pairs == 2:
                    column = columns[:, source * 8 + place : source * 8 + place + 1]
                else:
                    column = jnp.where(
                        pair == 1,
                        columns[:, source * 8 + 1 : source * 8 + 2],
                        columns[:, source * 8 : source * 8 + 1],
                    )
                total = total + column * landed[source, item, place].astype(jnp.float32)
            gathered[first + item, pair + place, pl.ds(pl.multiple_of(row, 16), rows)] = (
                total.astype(jnp.bfloat16)
            )

    def spread(delta):
        peer = lax.rem(rank + delta, mp_count)
        view = gathered.at[
            pl.ds(first, each), pl.ds(pair, pairs), pl.ds(pl.multiple_of(row, 16), rows)
        ]
        return pltpu.make_async_remote_copy(
            src_ref=view,
            dst_ref=view,
            send_sem=spread_send.at[delta],
            recv_sem=spread_recv.at[delta],
            device_id={"mp": peer},
            device_id_type=MESH,
        )

    for delta in range(1, mp_count):
        spread(delta).start()
    for delta in range(1, mp_count):
        spread(delta).wait()

    def drain(turn, carry):
        for target in range(dp_count * share):

            @pl.when(away(turn, target))
            def _():
                for copy in sends(turn, target):
                    copy.wait_send()

        return carry

    lax.fori_loop(0, prompts, drain, 0)
    out_ref[...] = gathered[...]


def attend(query, prompt_keys, prompt_values, extra_keys, extra_values, mask, dp_count, mp_count):
    prompts, pairs, rows, _ = query.shape
    count = dp_count * mp_count
    _, each, _, some_pairs, _, some_rows = region(0, prompts, mp_count)
    targets = dp_count * max(1, mp_count // prompts)
    vmem = pl.BlockSpec(memory_space=pltpu.VMEM)
    hbm = pl.BlockSpec(memory_space=pl.ANY)
    dma = pltpu.SemaphoreType.DMA
    merged = (prompts, pairs, rows // dp_count, HD)
    return pl.pallas_call(
        functools.partial(attend_kernel, dp_count, mp_count),
        out_shape=jax.ShapeDtypeStruct(merged, jnp.bfloat16),
        in_specs=[vmem, hbm, hbm, vmem, vmem, vmem],
        out_specs=vmem,
        scratch_shapes=[
            pltpu.VMEM((2,) + prompt_keys.shape[1:], jnp.bfloat16),
            pltpu.VMEM((2,) + prompt_values.shape[1:], jnp.bfloat16),
            pltpu.VMEM((prompts, pairs, rows, HD), jnp.bfloat16),
            pltpu.VMEM((prompts, 8, rows), jnp.float32),
            pltpu.VMEM((count, each, some_pairs, some_rows, HD), jnp.bfloat16),
            pltpu.VMEM((count, each, 8, rows), jnp.float32),
            pltpu.VMEM((rows, count * 8), jnp.float32),
            pltpu.VMEM(merged, jnp.bfloat16),
            dma((2,)),
            dma((2,)),
            dma((prompts, targets)),
            dma((count, each)),
            dma((prompts, targets)),
            dma((count, each)),
            dma((mp_count,)),
            dma((mp_count,)),
        ],
        compiler_params=pltpu.CompilerParams(
            collective_id=1, has_side_effects=True, vmem_limit_bytes=VMEM_LIMIT
        ),
        name="attend",
    )(query, prompt_keys, prompt_values, extra_keys, extra_values, mask)


def lineage(parents, step, stop):
    beams = parents.shape[2]
    source = jnp.broadcast_to(jnp.arange(beams, dtype=jnp.int32)[None, :], parents.shape[1:])
    for later in range(step, stop, -1):
        choice = source[:, :, None] == jnp.arange(beams, dtype=jnp.int32)
        source = jnp.sum(jnp.where(choice, parents[later][:, None, :], 0), axis=-1)
    return source


def on_device(
    hidden,
    gain,
    w_query,
    w_key,
    w_value,
    query_bias,
    key_bias,
    value_bias,
    w_out,
    prompt_keys,
    prompt_values,
    gen_keys,
    gen_values,
    parents,
):
    beam = lax.axis_index("dp")
    rank = lax.axis_index("mp")
    beams = lax.axis_size("dp")
    mp_count = lax.axis_size("mp")
    steps, prompts = hidden.shape[:2]
    rows = steps * prompts
    per_rank = -(-HEADS // mp_count)

    widened = hidden.reshape(rows, -1).astype(jnp.float32)
    squares = jnp.sum(widened * widened, axis=-1, keepdims=True)
    scaled = (widened * gain).astype(jnp.bfloat16)
    partial = [
        jnp.dot(scaled, weight, preferred_element_type=jnp.float32)
        for weight in (w_query, w_key, w_value)
    ]
    bias = jnp.concatenate([query_bias, key_bias, value_bias]).reshape(HEADS, HD)
    bias = jnp.pad(bias, ((0, per_rank * mp_count - HEADS), (0, 0)))
    projected = exchange(
        *partial, jnp.broadcast_to(squares, (rows, HD)), bias, beams, mp_count, per_rank
    )

    query = projected[:, :QH].reshape(beams, 2, 2, REPEAT, steps, prompts, HD)
    query = query.transpose(5, 1, 0, 2, 4, 3, 6)
    split = jnp.arange(2)
    same = (split[:, None] == split[None, :])[None, None, None, :, None, None, :, None]
    query = jnp.where(same, query[:, :, :, :, :, :, None, :], jnp.bfloat16(0))
    query = query.reshape(prompts, 2, beams * 2 * steps * REPEAT, 2 * HD)

    own = lax.dynamic_index_in_dim(projected, beam, 0, keepdims=False)
    fresh = own[QH:HEADS].reshape(2, KVH, steps, prompts, HD).transpose(0, 3, 2, 1, 4)
    fresh = fresh.reshape(2, prompts, steps, KVH * HD)
    width = gen_keys.shape[2]
    extras = -(-(width + steps) // 16) * 16
    pad = jnp.zeros((prompts, extras - width - steps, KVH * HD), jnp.bfloat16)
    extra_keys = jnp.concatenate([gen_keys[:, 0], fresh[0], pad], axis=1)
    extra_values = jnp.concatenate([gen_values[:, 0], fresh[1], pad], axis=1)

    seen = []
    for step in range(steps):
        anchor = lineage(parents, step, -1) == beam
        columns = [jnp.broadcast_to(anchor[:, :, None], (prompts, beams, width))]
        for source in range(steps):
            if source <= step:
                flag = (lineage(parents, step, source) == beam) & (rank == 0)
            else:
                flag = jnp.zeros((prompts, beams), jnp.bool_)
            columns.append(flag[:, :, None])
        columns.append(jnp.zeros((prompts, beams, extras - width - steps), jnp.bool_))
        seen.append(jnp.concatenate(columns, axis=2))
    mask = jnp.where(jnp.stack(seen, axis=2), jnp.float32(0), jnp.float32(hidden_fill))
    mask = jnp.broadcast_to(
        mask[:, :, None, :, None, :], (prompts, beams, 2, steps, REPEAT, extras)
    ).reshape(prompts, beams * 2 * steps * REPEAT, extras)

    attended = attend(
        query, prompt_keys, prompt_values, extra_keys, extra_values, mask, beams, mp_count
    )
    attended = attended.reshape(prompts, 2, 2, steps, REPEAT, HD).transpose(3, 0, 1, 2, 4, 5)
    attended = attended.reshape(rows, QH * HD)
    result = jnp.dot(attended, w_out, preferred_element_type=jnp.float32).astype(jnp.bfloat16)
    return result.reshape(steps, prompts, 1, -1)


def solution(mesh):
    return jax.shard_map(
        on_device,
        mesh=mesh,
        in_specs=(
            P(None, "groups", "dp", "mp"),
            P("mp"),
            P("mp", None),
            P("mp", None),
            P("mp", None),
            P(),
            P(),
            P(),
            P(None, "mp"),
            P("groups", ("dp", "mp"), None),
            P("groups", ("dp", "mp"), None),
            P("groups", "dp", "mp", None),
            P("groups", "dp", "mp", None),
            P(None, "groups", None),
        ),
        out_specs=P(None, "groups", "dp", "mp"),
        check_vma=False,
    )
```

```python
import functools

import jax
import jax.numpy as jnp
from jax import lax
from jax.experimental import pallas as pl
from jax.experimental.pallas import tpu as pltpu
from jax.sharding import PartitionSpec as P

D = 8192
QH = 32
KVH = 4
HD = 128
REPEAT = QH // KVH
MESH = pl.DeviceIdType.MESH
VMEM_LIMIT = 60 * 1024 * 1024
hidden_fill = -1e30


def exchange_kernel(
    dp_count,
    mp_count,
    per_rank,
    scaled_ref,
    query_hbm,
    key_hbm,
    value_hbm,
    squares_ref,
    bias_ref,
    out_ref,
    query_slots,
    key_slots,
    value_slots,
    query_sem,
    key_sem,
    value_sem,
    parts,
    landed,
    gathered,
    reduce_send,
    reduce_recv,
    spread_send,
    spread_recv,
    far_send,
    far_recv,
    near_send,
    near_recv,
):
    beam = lax.axis_index("dp")
    rank = lax.axis_index("mp")
    far = lax.rem(beam + dp_count // 2, dp_count)
    near = beam + 1 - 2 * lax.rem(beam, 2)

    slots = query_slots.shape[0]
    query_width = query_slots.shape[2]

    def weights(step):
        owner = lax.rem(rank + step + 1, mp_count)
        narrow = jnp.minimum(owner, KVH - 1)
        slot = step % slots
        wide = pl.ds(pl.multiple_of(owner * query_width, HD), query_width)
        head = pl.ds(pl.multiple_of(narrow * HD, HD), HD)
        return (
            pltpu.make_async_copy(
                query_hbm.at[:, wide], query_slots.at[slot], query_sem.at[slot]
            ),
            pltpu.make_async_copy(key_hbm.at[:, head], key_slots.at[slot], key_sem.at[slot]),
            pltpu.make_async_copy(value_hbm.at[:, head], value_slots.at[slot], value_sem.at[slot]),
        )

    for step in range(slots):
        for copy in weights(step):
            copy.start()

    barrier = pltpu.get_barrier_semaphore()
    for delta in range(1, mp_count):
        pl.semaphore_signal(
            barrier,
            inc=1,
            device_id={"mp": lax.rem(rank + delta, mp_count)},
            device_id_type=MESH,
        )
    for partner in (far, near):
        pl.semaphore_signal(barrier, inc=1, device_id={"dp": partner}, device_id_type=MESH)

    pl.semaphore_wait(barrier, mp_count + 1)

    def reduce_copy(delta):
        peer = lax.rem(rank + delta, mp_count)
        return pltpu.make_async_remote_copy(
            src_ref=parts.at[peer],
            dst_ref=landed.at[delta],
            send_sem=reduce_send.at[delta],
            recv_sem=reduce_recv.at[delta],
            device_id={"mp": peer},
            device_id_type=MESH,
        )

    scaled = scaled_ref[...]
    places = query_width // HD
    for step in range(mp_count):
        owner = lax.rem(rank + step + 1, mp_count)
        slot = step % slots
        for copy in weights(step):
            copy.wait()
        product = jnp.dot(scaled, query_slots[slot], preferred_element_type=jnp.float32)
        for place in range(places):
            parts[owner, place] = product[:, place * HD : (place + 1) * HD]
        parts[owner, places] = jnp.dot(
            scaled, key_slots[slot], preferred_element_type=jnp.float32
        )
        parts[owner, places + 1] = jnp.dot(
            scaled, value_slots[slot], preferred_element_type=jnp.float32
        )
        parts[owner, per_rank] = squares_ref[...]
        if step + slots < mp_count:
            for copy in weights(step + slots):
                copy.start()
        if step < mp_count - 1:
            reduce_copy(step + 1).start()
    total = parts[rank]
    for delta in range(1, mp_count):
        reduce_copy(delta).wait_recv()
        total = total + landed[delta]
    inverse = lax.rsqrt(total[per_rank] / D + 1e-06)
    mine = pl.ds(rank * per_rank, per_rank)
    done = total[:per_rank] * inverse[None] + bias_ref[mine][:, None, :]
    gathered[beam, mine] = done.astype(jnp.bfloat16)

    def spread_copy(delta):
        peer = lax.rem(rank + delta, mp_count)
        return pltpu.make_async_remote_copy(
            src_ref=gathered.at[beam, mine],
            dst_ref=gathered.at[beam, mine],
            send_sem=spread_send.at[delta],
            recv_sem=spread_recv.at[delta],
            device_id={"mp": peer},
            device_id_type=MESH,
        )

    def dp_copy(delta, source_beam, partner, send, recv, slot):
        owner = lax.rem(rank - delta + mp_count, mp_count)
        block = pl.ds(owner * per_rank, per_rank)
        return pltpu.make_async_remote_copy(
            src_ref=gathered.at[source_beam, block],
            dst_ref=gathered.at[source_beam, block],
            send_sem=send.at[slot, delta],
            recv_sem=recv.at[slot, delta],
            device_id={"dp": partner},
            device_id_type=MESH,
        )

    for delta in range(1, mp_count):
        spread_copy(delta).start()
    for delta in range(mp_count):
        if delta:
            spread_copy(delta).wait_recv()
        dp_copy(delta, beam, far, far_send, far_recv, 0).start()
        dp_copy(delta, beam, near, near_send, near_recv, 0).start()
    for delta in range(mp_count):
        dp_copy(delta, beam, far, far_send, far_recv, 0).wait_recv()
        dp_copy(delta, far, near, near_send, near_recv, 1).start()
    for delta in range(mp_count):
        dp_copy(delta, beam, near, near_send, near_recv, 0).wait_recv()
        dp_copy(delta, far, near, near_send, near_recv, 1).wait_recv()
    for delta in range(mp_count):
        if delta:
            reduce_copy(delta).wait_send()
            spread_copy(delta).wait_send()
        dp_copy(delta, beam, far, far_send, far_recv, 0).wait_send()
        dp_copy(delta, beam, near, near_send, near_recv, 0).wait_send()
        dp_copy(delta, far, near, near_send, near_recv, 1).wait_send()
    out_ref[...] = gathered[...]


def exchange(scaled, query, key, value, squares, bias, dp_count, mp_count, per_rank):
    rows = squares.shape[0]
    heads = mp_count * per_rank
    depth = query.shape[0]
    slots = min(mp_count, 3)
    vmem = pl.BlockSpec(memory_space=pltpu.VMEM)
    hbm = pl.BlockSpec(memory_space=pl.ANY)
    dma = pltpu.SemaphoreType.DMA
    return pl.pallas_call(
        functools.partial(exchange_kernel, dp_count, mp_count, per_rank),
        out_shape=jax.ShapeDtypeStruct((dp_count, heads, rows, HD), jnp.bfloat16),
        in_specs=[vmem, hbm, hbm, hbm, vmem, vmem],
        out_specs=vmem,
        scratch_shapes=[
            pltpu.VMEM((slots, depth, query.shape[1] // mp_count), jnp.bfloat16),
            pltpu.VMEM((slots, depth, HD), jnp.bfloat16),
            pltpu.VMEM((slots, depth, HD), jnp.bfloat16),
            dma((slots,)),
            dma((slots,)),
            dma((slots,)),
            pltpu.VMEM((mp_count, per_rank + 1, rows, HD), jnp.float32),
            pltpu.VMEM((mp_count, per_rank + 1, rows, HD), jnp.float32),
            pltpu.VMEM((dp_count, heads, rows, HD), jnp.bfloat16),
            dma((mp_count,)),
            dma((mp_count,)),
            dma((mp_count,)),
            dma((mp_count,)),
            dma((1, mp_count)),
            dma((1, mp_count)),
            dma((2, mp_count)),
            dma((2, mp_count)),
        ],
        compiler_params=pltpu.CompilerParams(
            collective_id=0, has_side_effects=True, vmem_limit_bytes=VMEM_LIMIT
        ),
        name="exchange",
    )(scaled, query, key, value, squares, bias)


def region(rank, prompts, mp_count):
    if mp_count <= prompts:
        each = prompts // mp_count
        return rank * each, each, 0, 2, 0, 32
    share = mp_count // prompts
    place = lax.rem(rank, share)
    if share == 2:
        return rank // share, 1, place, 1, 0, 32
    return rank // share, 1, place // 2, 1, lax.rem(place, 2) * 16, 16


def attend_kernel(
    dp_count,
    mp_count,
    query_ref,
    key_hbm,
    value_hbm,
    extra_key_ref,
    extra_value_ref,
    mask_ref,
    out_ref,
    keys,
    values,
    outs,
    stats,
    landed,
    landed_stats,
    flipped,
    gathered,
    key_sem,
    value_sem,
    out_send,
    out_recv,
    stat_send,
    stat_recv,
    spread_send,
    spread_recv,
):
    beam = lax.axis_index("dp")
    rank = lax.axis_index("mp")
    count = dp_count * mp_count
    me = beam * mp_count + rank
    prompts, pairs_all, wide_rows, wide = query_ref.shape
    beam_rows = wide_rows // dp_count
    share = max(1, mp_count // prompts)
    each = max(1, prompts // mp_count)
    factor = HD ** (-0.5)
    contract_last = (((1,), (1,)), ((), ()))
    origin = rank * each // share + each

    def place_of(turn):
        return lax.rem(origin + turn, prompts)

    def loads(turn):
        prompt = place_of(turn)
        slot = lax.rem(turn, 2)
        return (
            pltpu.make_async_copy(key_hbm.at[prompt], keys.at[slot], key_sem.at[slot]),
            pltpu.make_async_copy(value_hbm.at[prompt], values.at[slot], value_sem.at[slot]),
        )

    for copy in loads(0):
        copy.start()

    barrier = pltpu.get_barrier_semaphore()

    def greet(delta, carry):
        peer = lax.rem(me + delta, count)
        pl.semaphore_signal(
            barrier,
            inc=1,
            device_id={"dp": peer // mp_count, "mp": lax.rem(peer, mp_count)},
            device_id_type=MESH,
        )
        return carry

    lax.fori_loop(1, count, greet, 0)
    stats[...] = jnp.zeros_like(stats)
    pl.semaphore_wait(barrier, count - 1)

    def owner_of(turn, target):
        prompt = place_of(turn)
        if share > 1:
            return prompt * share + lax.rem(target, share)
        return prompt // each

    def sends(turn, target):
        prompt = place_of(turn)
        owner = owner_of(turn, target)
        other = target // share
        _, _, pair, pairs, row, rows = region(owner, prompts, mp_count)
        item = lax.rem(prompt, each)
        start = pl.multiple_of(other * beam_rows + row, 16)
        where = {"dp": other, "mp": owner}
        return (
            pltpu.make_async_remote_copy(
                src_ref=outs.at[prompt, pl.ds(pair, pairs), pl.ds(start, rows)],
                dst_ref=landed.at[me, item],
                send_sem=out_send.at[turn, target],
                recv_sem=out_recv.at[me, item],
                device_id=where,
                device_id_type=MESH,
            ),
            pltpu.make_async_remote_copy(
                src_ref=stats.at[prompt],
                dst_ref=landed_stats.at[me, item],
                send_sem=stat_send.at[turn, target],
                recv_sem=stat_recv.at[me, item],
                device_id=where,
                device_id_type=MESH,
            ),
        )

    def away(turn, target):
        return (target // share) * mp_count + owner_of(turn, target) != me

    row_id = lax.broadcasted_iota(jnp.int32, (wide_rows, HD), 0)
    second = lax.rem(row_id // (wide_rows // 8), 2) == 1

    def work(turn, carry):
        prompt = place_of(turn)
        slot = lax.rem(turn, 2)

        @pl.when(turn + 1 < prompts)
        def _():
            for copy in loads(turn + 1):
                copy.start()

        for copy in loads(turn):
            copy.wait()
        for pair in range(pairs_all):
            lanes = slice(pair * wide, (pair + 1) * wide)
            query = query_ref[prompt, pair]
            scores = lax.dot_general(
                query, keys[slot, :, lanes], contract_last, preferred_element_type=jnp.float32
            )
            extra = lax.dot_general(
                query,
                extra_key_ref[prompt, :, lanes],
                contract_last,
                preferred_element_type=jnp.float32,
            )
            extra = extra + mask_ref[prompt]
            top = jnp.maximum(
                jnp.max(scores, axis=-1, keepdims=True), jnp.max(extra, axis=-1, keepdims=True)
            )
            weights = jnp.exp((scores - top) * factor)
            extra_weights = jnp.exp((extra - top) * factor)
            total = jnp.sum(weights, axis=-1, keepdims=True) + jnp.sum(
                extra_weights, axis=-1, keepdims=True
            )
            numerator = jnp.dot(
                weights.astype(jnp.bfloat16),
                values[slot, :, lanes],
                preferred_element_type=jnp.float32,
            ) + jnp.dot(
                extra_weights.astype(jnp.bfloat16),
                extra_value_ref[prompt, :, lanes],
                preferred_element_type=jnp.float32,
            )
            own = jnp.where(second, numerator[:, HD:], numerator[:, :HD])
            outs[prompt, pair] = (own / total).astype(jnp.bfloat16)
            level = top * factor + jnp.log(total)
            flat = jnp.transpose(jnp.broadcast_to(level, (wide_rows, HD)))
            stats[prompt, pair : pair + 1] = flat[:1]
        for target in range(dp_count * share):

            @pl.when(away(turn, target))
            def _():
                for copy in sends(turn, target):
                    copy.start()

        return carry

    lax.fori_loop(0, prompts, work, 0)

    first, _, pair, pairs, row, rows = region(rank, prompts, mp_count)
    start = pl.multiple_of(beam * beam_rows + row, 16)
    landed[me] = outs[pl.ds(first, each), pl.ds(pair, pairs), pl.ds(start, rows)]
    landed_stats[me] = stats[pl.ds(first, each)]

    def finish(delta, carry):
        peer = lax.rem(me + delta, count)
        for item in range(each):
            pltpu.make_async_remote_copy(
                src_ref=landed.at[me, item],
                dst_ref=landed.at[peer, item],
                send_sem=out_send.at[0, 0],
                recv_sem=out_recv.at[peer, item],
                device_id={"dp": peer // mp_count, "mp": lax.rem(peer, mp_count)},
                device_id_type=MESH,
            ).wait_recv()
            pltpu.make_async_remote_copy(
                src_ref=landed_stats.at[me, item],
                dst_ref=landed_stats.at[peer, item],
                send_sem=stat_send.at[0, 0],
                recv_sem=stat_recv.at[peer, item],
                device_id={"dp": peer // mp_count, "mp": lax.rem(peer, mp_count)},
                device_id_type=MESH,
            ).wait_recv()
        return carry

    lax.fori_loop(1, count, finish, 0)

    for item in range(each):
        levels = landed_stats[:, item]
        top = jnp.max(levels, axis=0, keepdims=True)
        shares = jnp.exp(levels - top)
        shares = shares / jnp.sum(shares, axis=0, keepdims=True)
        flipped[...] = jnp.transpose(shares.reshape(count * 8, shares.shape[-1]))
        columns = flipped[pl.ds(start, rows), :]
        for place in range(pairs):
            total = jnp.zeros((rows, HD), jnp.float32)
            for source in range(count):
                if pairs == 2:
                    column = columns[:, source * 8 + place : source * 8 + place + 1]
                else:
                    column = jnp.where(
                        pair == 1,
                        columns[:, source * 8 + 1 : source * 8 + 2],
                        columns[:, source * 8 : source * 8 + 1],
                    )
                total = total + column * landed[source, item, place].astype(jnp.float32)
            gathered[first + item, pair + place, pl.ds(pl.multiple_of(row, 16), rows)] = (
                total.astype(jnp.bfloat16)
            )

    def spread(delta):
        peer = lax.rem(rank + delta, mp_count)
        view = gathered.at[
            pl.ds(first, each), pl.ds(pair, pairs), pl.ds(pl.multiple_of(row, 16), rows)
        ]
        return pltpu.make_async_remote_copy(
            src_ref=view,
            dst_ref=view,
            send_sem=spread_send.at[delta],
            recv_sem=spread_recv.at[delta],
            device_id={"mp": peer},
            device_id_type=MESH,
        )

    for delta in range(1, mp_count):
        spread(delta).start()
    for delta in range(1, mp_count):
        spread(delta).wait()

    def drain(turn, carry):
        for target in range(dp_count * share):

            @pl.when(away(turn, target))
            def _():
                for copy in sends(turn, target):
                    copy.wait_send()

        return carry

    lax.fori_loop(0, prompts, drain, 0)
    out_ref[...] = gathered[...]


def attend(query, prompt_keys, prompt_values, extra_keys, extra_values, mask, dp_count, mp_count):
    prompts, pairs, rows, _ = query.shape
    count = dp_count * mp_count
    _, each, _, some_pairs, _, some_rows = region(0, prompts, mp_count)
    targets = dp_count * max(1, mp_count // prompts)
    vmem = pl.BlockSpec(memory_space=pltpu.VMEM)
    hbm = pl.BlockSpec(memory_space=pl.ANY)
    dma = pltpu.SemaphoreType.DMA
    merged = (prompts, pairs, rows // dp_count, HD)
    return pl.pallas_call(
        functools.partial(attend_kernel, dp_count, mp_count),
        out_shape=jax.ShapeDtypeStruct(merged, jnp.bfloat16),
        in_specs=[vmem, hbm, hbm, vmem, vmem, vmem],
        out_specs=vmem,
        scratch_shapes=[
            pltpu.VMEM((2,) + prompt_keys.shape[1:], jnp.bfloat16),
            pltpu.VMEM((2,) + prompt_values.shape[1:], jnp.bfloat16),
            pltpu.VMEM((prompts, pairs, rows, HD), jnp.bfloat16),
            pltpu.VMEM((prompts, 8, rows), jnp.float32),
            pltpu.VMEM((count, each, some_pairs, some_rows, HD), jnp.bfloat16),
            pltpu.VMEM((count, each, 8, rows), jnp.float32),
            pltpu.VMEM((rows, count * 8), jnp.float32),
            pltpu.VMEM(merged, jnp.bfloat16),
            dma((2,)),
            dma((2,)),
            dma((prompts, targets)),
            dma((count, each)),
            dma((prompts, targets)),
            dma((count, each)),
            dma((mp_count,)),
            dma((mp_count,)),
        ],
        compiler_params=pltpu.CompilerParams(
            collective_id=1, has_side_effects=True, vmem_limit_bytes=VMEM_LIMIT
        ),
        name="attend",
    )(query, prompt_keys, prompt_values, extra_keys, extra_values, mask)


def lineage(parents, step, stop):
    beams = parents.shape[2]
    source = jnp.broadcast_to(jnp.arange(beams, dtype=jnp.int32)[None, :], parents.shape[1:])
    for later in range(step, stop, -1):
        choice = source[:, :, None] == jnp.arange(beams, dtype=jnp.int32)
        source = jnp.sum(jnp.where(choice, parents[later][:, None, :], 0), axis=-1)
    return source


def on_device(
    hidden,
    gain,
    w_query,
    w_key,
    w_value,
    query_bias,
    key_bias,
    value_bias,
    w_out,
    prompt_keys,
    prompt_values,
    gen_keys,
    gen_values,
    parents,
):
    beam = lax.axis_index("dp")
    rank = lax.axis_index("mp")
    beams = lax.axis_size("dp")
    mp_count = lax.axis_size("mp")
    steps, prompts = hidden.shape[:2]
    rows = steps * prompts
    per_rank = QH // mp_count + 2

    widened = hidden.reshape(rows, -1).astype(jnp.float32)
    squares = jnp.sum(widened * widened, axis=-1, keepdims=True)
    scaled = (widened * gain).astype(jnp.bfloat16)
    places = QH // mp_count
    narrow = [min(owner, KVH - 1) for owner in range(mp_count)]
    narrow_bias = [
        jnp.stack([array[head * HD : (head + 1) * HD] for head in narrow])[:, None]
        for array in (key_bias, value_bias)
    ]
    bias = jnp.concatenate([query_bias.reshape(mp_count, places, HD)] + narrow_bias, axis=1)
    projected = exchange(
        scaled,
        w_query,
        w_key,
        w_value,
        jnp.broadcast_to(squares, (rows, HD)),
        bias.reshape(mp_count * per_rank, HD),
        beams,
        mp_count,
        per_rank,
    ).reshape(beams, mp_count, per_rank, rows, HD)

    query = projected[:, :, :places].reshape(beams, 2, 2, REPEAT, steps, prompts, HD)
    query = query.transpose(5, 1, 0, 2, 4, 3, 6)
    split = jnp.arange(2)
    same = (split[:, None] == split[None, :])[None, None, None, :, None, None, :, None]
    query = jnp.where(same, query[:, :, :, :, :, :, None, :], jnp.bfloat16(0))
    query = query.reshape(prompts, 2, beams * 2 * steps * REPEAT, 2 * HD)

    own = lax.dynamic_index_in_dim(projected, beam, 0, keepdims=False)
    fresh = own[:KVH, places:].reshape(KVH, 2, steps, prompts, HD).transpose(1, 3, 2, 0, 4)
    fresh = fresh.reshape(2, prompts, steps, KVH * HD)
    width = gen_keys.shape[2]
    extras = -(-(width + steps) // 16) * 16
    pad = jnp.zeros((prompts, extras - width - steps, KVH * HD), jnp.bfloat16)
    extra_keys = jnp.concatenate([gen_keys[:, 0], fresh[0], pad], axis=1)
    extra_values = jnp.concatenate([gen_values[:, 0], fresh[1], pad], axis=1)

    seen = []
    for step in range(steps):
        anchor = lineage(parents, step, -1) == beam
        columns = [jnp.broadcast_to(anchor[:, :, None], (prompts, beams, width))]
        for source in range(steps):
            if source <= step:
                flag = (lineage(parents, step, source) == beam) & (rank == 0)
            else:
                flag = jnp.zeros((prompts, beams), jnp.bool_)
            columns.append(flag[:, :, None])
        columns.append(jnp.zeros((prompts, beams, extras - width - steps), jnp.bool_))
        seen.append(jnp.concatenate(columns, axis=2))
    mask = jnp.where(jnp.stack(seen, axis=2), jnp.float32(0), jnp.float32(hidden_fill))
    mask = jnp.broadcast_to(
        mask[:, :, None, :, None, :], (prompts, beams, 2, steps, REPEAT, extras)
    ).reshape(prompts, beams * 2 * steps * REPEAT, extras)

    attended = attend(
        query, prompt_keys, prompt_values, extra_keys, extra_values, mask, beams, mp_count
    )
    attended = attended.reshape(prompts, 2, 2, steps, REPEAT, HD).transpose(3, 0, 1, 2, 4, 5)
    attended = attended.reshape(rows, QH * HD)
    result = jnp.dot(attended, w_out, preferred_element_type=jnp.float32).astype(jnp.bfloat16)
    return result.reshape(steps, prompts, 1, -1)


def solution(mesh):
    return jax.shard_map(
        on_device,
        mesh=mesh,
        in_specs=(
            P(None, "groups", "dp", "mp"),
            P("mp"),
            P("mp", None),
            P("mp", None),
            P("mp", None),
            P(),
            P(),
            P(),
            P(None, "mp"),
            P("groups", ("dp", "mp"), None),
            P("groups", ("dp", "mp"), None),
            P("groups", "dp", "mp", None),
            P("groups", "dp", "mp", None),
            P(None, "groups", None),
        ),
        out_specs=P(None, "groups", "dp", "mp"),
        check_vma=False,
    )
```

```python
import functools

import jax
import jax.numpy as jnp
from jax import lax
from jax.experimental import pallas as pl
from jax.experimental.pallas import tpu as pltpu
from jax.sharding import PartitionSpec as P

D = 8192
QH = 32
KVH = 4
HD = 128
REPEAT = QH // KVH
MESH = pl.DeviceIdType.MESH
VMEM_LIMIT = 48 * 1024 * 1024
hidden_fill = -1e30


def exchange_kernel(
    dp_count,
    mp_count,
    per_rank,
    scaled_ref,
    query_hbm,
    key_hbm,
    value_hbm,
    squares_ref,
    bias_ref,
    out_ref,
    query_slots,
    key_slots,
    value_slots,
    query_sem,
    key_sem,
    value_sem,
    parts,
    landed,
    gathered,
    reduce_send,
    reduce_recv,
    spread_send,
    spread_recv,
    far_send,
    far_recv,
    near_send,
    near_recv,
):
    beam = lax.axis_index("dp")
    rank = lax.axis_index("mp")
    far = lax.rem(beam + dp_count // 2, dp_count)
    near = beam + 1 - 2 * lax.rem(beam, 2)

    slots = query_slots.shape[0]
    query_width = query_slots.shape[2]

    def weights(step):
        owner = lax.rem(rank + step + 1, mp_count)
        narrow = jnp.minimum(owner, KVH - 1)
        slot = step % slots
        wide = pl.ds(pl.multiple_of(owner * query_width, HD), query_width)
        head = pl.ds(pl.multiple_of(narrow * HD, HD), HD)
        return (
            pltpu.make_async_copy(
                query_hbm.at[:, wide], query_slots.at[slot], query_sem.at[slot]
            ),
            pltpu.make_async_copy(key_hbm.at[:, head], key_slots.at[slot], key_sem.at[slot]),
            pltpu.make_async_copy(value_hbm.at[:, head], value_slots.at[slot], value_sem.at[slot]),
        )

    for step in range(slots):
        for copy in weights(step):
            copy.start()

    barrier = pltpu.get_barrier_semaphore()
    for delta in range(1, mp_count):
        pl.semaphore_signal(
            barrier,
            inc=1,
            device_id={"mp": lax.rem(rank + delta, mp_count)},
            device_id_type=MESH,
        )
    for partner in (far, near):
        pl.semaphore_signal(barrier, inc=1, device_id={"dp": partner}, device_id_type=MESH)

    pl.semaphore_wait(barrier, mp_count + 1)

    def reduce_copy(delta):
        peer = lax.rem(rank + delta, mp_count)
        return pltpu.make_async_remote_copy(
            src_ref=parts.at[peer],
            dst_ref=landed.at[delta],
            send_sem=reduce_send.at[delta],
            recv_sem=reduce_recv.at[delta],
            device_id={"mp": peer},
            device_id_type=MESH,
        )

    scaled = scaled_ref[...]
    places = query_width // HD
    for step in range(mp_count):
        owner = lax.rem(rank + step + 1, mp_count)
        slot = step % slots
        for copy in weights(step):
            copy.wait()
        product = jnp.dot(scaled, query_slots[slot], preferred_element_type=jnp.float32)
        for place in range(places):
            parts[owner, place] = product[:, place * HD : (place + 1) * HD]
        parts[owner, places] = jnp.dot(
            scaled, key_slots[slot], preferred_element_type=jnp.float32
        )
        parts[owner, places + 1] = jnp.dot(
            scaled, value_slots[slot], preferred_element_type=jnp.float32
        )
        parts[owner, per_rank] = squares_ref[...]
        if step + slots < mp_count:
            for copy in weights(step + slots):
                copy.start()
        if step < mp_count - 1:
            reduce_copy(step + 1).start()
    total = parts[rank]
    for delta in range(1, mp_count):
        reduce_copy(delta).wait_recv()
        total = total + landed[delta]
    inverse = lax.rsqrt(total[per_rank] / D + 1e-06)
    mine = pl.ds(rank * per_rank, per_rank)
    done = total[:per_rank] * inverse[None] + bias_ref[mine][:, None, :]
    gathered[beam, mine] = done.astype(jnp.bfloat16)

    def spread_copy(delta):
        peer = lax.rem(rank + delta, mp_count)
        return pltpu.make_async_remote_copy(
            src_ref=gathered.at[beam, mine],
            dst_ref=gathered.at[beam, mine],
            send_sem=spread_send.at[delta],
            recv_sem=spread_recv.at[delta],
            device_id={"mp": peer},
            device_id_type=MESH,
        )

    def dp_copy(delta, source_beam, partner, send, recv, slot):
        owner = lax.rem(rank - delta + mp_count, mp_count)
        block = pl.ds(owner * per_rank, per_rank)
        return pltpu.make_async_remote_copy(
            src_ref=gathered.at[source_beam, block],
            dst_ref=gathered.at[source_beam, block],
            send_sem=send.at[slot, delta],
            recv_sem=recv.at[slot, delta],
            device_id={"dp": partner},
            device_id_type=MESH,
        )

    for delta in range(1, mp_count):
        spread_copy(delta).start()
    for delta in range(mp_count):
        if delta:
            spread_copy(delta).wait_recv()
        dp_copy(delta, beam, far, far_send, far_recv, 0).start()
        dp_copy(delta, beam, near, near_send, near_recv, 0).start()
    for delta in range(mp_count):
        dp_copy(delta, beam, far, far_send, far_recv, 0).wait_recv()
        dp_copy(delta, far, near, near_send, near_recv, 1).start()
    for delta in range(mp_count):
        dp_copy(delta, beam, near, near_send, near_recv, 0).wait_recv()
        dp_copy(delta, far, near, near_send, near_recv, 1).wait_recv()
    for delta in range(mp_count):
        if delta:
            reduce_copy(delta).wait_send()
            spread_copy(delta).wait_send()
        dp_copy(delta, beam, far, far_send, far_recv, 0).wait_send()
        dp_copy(delta, beam, near, near_send, near_recv, 0).wait_send()
        dp_copy(delta, far, near, near_send, near_recv, 1).wait_send()
    out_ref[...] = gathered[...]


def exchange(scaled, query, key, value, squares, bias, dp_count, mp_count, per_rank):
    rows = squares.shape[0]
    heads = mp_count * per_rank
    depth = query.shape[0]
    slots = min(mp_count, 3)
    vmem = pl.BlockSpec(memory_space=pltpu.VMEM)
    hbm = pl.BlockSpec(memory_space=pl.ANY)
    dma = pltpu.SemaphoreType.DMA
    return pl.pallas_call(
        functools.partial(exchange_kernel, dp_count, mp_count, per_rank),
        out_shape=jax.ShapeDtypeStruct((dp_count, heads, rows, HD), jnp.bfloat16),
        in_specs=[vmem, hbm, hbm, hbm, vmem, vmem],
        out_specs=vmem,
        scratch_shapes=[
            pltpu.VMEM((slots, depth, query.shape[1] // mp_count), jnp.bfloat16),
            pltpu.VMEM((slots, depth, HD), jnp.bfloat16),
            pltpu.VMEM((slots, depth, HD), jnp.bfloat16),
            dma((slots,)),
            dma((slots,)),
            dma((slots,)),
            pltpu.VMEM((mp_count, per_rank + 1, rows, HD), jnp.float32),
            pltpu.VMEM((mp_count, per_rank + 1, rows, HD), jnp.float32),
            pltpu.VMEM((dp_count, heads, rows, HD), jnp.bfloat16),
            dma((mp_count,)),
            dma((mp_count,)),
            dma((mp_count,)),
            dma((mp_count,)),
            dma((1, mp_count)),
            dma((1, mp_count)),
            dma((2, mp_count)),
            dma((2, mp_count)),
        ],
        compiler_params=pltpu.CompilerParams(
            collective_id=0, has_side_effects=True, vmem_limit_bytes=VMEM_LIMIT
        ),
        name="exchange",
    )(scaled, query, key, value, squares, bias)


def region(rank, prompts, mp_count):
    if mp_count <= prompts:
        each = prompts // mp_count
        return rank * each, each, 0, 2, 0, 32
    share = mp_count // prompts
    place = lax.rem(rank, share)
    if share == 2:
        return rank // share, 1, place, 1, 0, 32
    return rank // share, 1, place // 2, 1, lax.rem(place, 2) * 16, 16


def attend_kernel(
    dp_count,
    mp_count,
    query_ref,
    key_hbm,
    value_hbm,
    extra_key_ref,
    extra_value_ref,
    mask_ref,
    out_ref,
    keys,
    values,
    outs,
    stats,
    landed,
    landed_stats,
    flipped,
    gathered,
    key_sem,
    value_sem,
    out_send,
    out_recv,
    stat_send,
    stat_recv,
    spread_send,
    spread_recv,
):
    beam = lax.axis_index("dp")
    rank = lax.axis_index("mp")
    count = dp_count * mp_count
    me = beam * mp_count + rank
    prompts, pairs_all, wide_rows, wide = query_ref.shape
    beam_rows = wide_rows // dp_count
    share = max(1, mp_count // prompts)
    each = max(1, prompts // mp_count)
    factor = HD ** (-0.5)
    contract_last = (((1,), (1,)), ((), ()))
    origin = rank * each // share + each

    def place_of(turn):
        return lax.rem(origin + turn, prompts)

    def loads(turn):
        prompt = place_of(turn)
        slot = lax.rem(turn, 2)
        return (
            pltpu.make_async_copy(key_hbm.at[prompt], keys.at[slot], key_sem.at[slot]),
            pltpu.make_async_copy(value_hbm.at[prompt], values.at[slot], value_sem.at[slot]),
        )

    for copy in loads(0):
        copy.start()

    barrier = pltpu.get_barrier_semaphore()

    def greet(delta, carry):
        peer = lax.rem(me + delta, count)
        pl.semaphore_signal(
            barrier,
            inc=1,
            device_id={"dp": peer // mp_count, "mp": lax.rem(peer, mp_count)},
            device_id_type=MESH,
        )
        return carry

    lax.fori_loop(1, count, greet, 0)
    stats[...] = jnp.zeros_like(stats)
    pl.semaphore_wait(barrier, count - 1)

    def owner_of(turn, target):
        prompt = place_of(turn)
        if share > 1:
            return prompt * share + lax.rem(target, share)
        return prompt // each

    def sends(turn, target):
        prompt = place_of(turn)
        owner = owner_of(turn, target)
        other = target // share
        _, _, pair, pairs, row, rows = region(owner, prompts, mp_count)
        item = lax.rem(prompt, each)
        start = pl.multiple_of(other * beam_rows + row, 16)
        where = {"dp": other, "mp": owner}
        return (
            pltpu.make_async_remote_copy(
                src_ref=outs.at[prompt, pl.ds(pair, pairs), pl.ds(start, rows)],
                dst_ref=landed.at[me, item],
                send_sem=out_send.at[turn, target],
                recv_sem=out_recv.at[me, item],
                device_id=where,
                device_id_type=MESH,
            ),
            pltpu.make_async_remote_copy(
                src_ref=stats.at[prompt],
                dst_ref=landed_stats.at[me, item],
                send_sem=stat_send.at[turn, target],
                recv_sem=stat_recv.at[me, item],
                device_id=where,
                device_id_type=MESH,
            ),
        )

    def away(turn, target):
        return (target // share) * mp_count + owner_of(turn, target) != me

    row_id = lax.broadcasted_iota(jnp.int32, (wide_rows, HD), 0)
    second = lax.rem(row_id // (wide_rows // 8), 2) == 1

    def work(turn, carry):
        prompt = place_of(turn)
        slot = lax.rem(turn, 2)

        @pl.when(turn + 1 < prompts)
        def _():
            for copy in loads(turn + 1):
                copy.start()

        for copy in loads(turn):
            copy.wait()
        for pair in range(pairs_all):
            lanes = slice(pair * wide, (pair + 1) * wide)
            query = query_ref[prompt, pair]
            scores = lax.dot_general(
                query, keys[slot, :, lanes], contract_last, preferred_element_type=jnp.float32
            )
            extra = lax.dot_general(
                query,
                extra_key_ref[prompt, :, lanes],
                contract_last,
                preferred_element_type=jnp.float32,
            )
            extra = extra + mask_ref[prompt]
            top = jnp.maximum(
                jnp.max(scores, axis=-1, keepdims=True), jnp.max(extra, axis=-1, keepdims=True)
            )
            weights = jnp.exp((scores - top) * factor)
            extra_weights = jnp.exp((extra - top) * factor)
            total = jnp.sum(weights, axis=-1, keepdims=True) + jnp.sum(
                extra_weights, axis=-1, keepdims=True
            )
            numerator = jnp.dot(
                weights.astype(jnp.bfloat16),
                values[slot, :, lanes],
                preferred_element_type=jnp.float32,
            ) + jnp.dot(
                extra_weights.astype(jnp.bfloat16),
                extra_value_ref[prompt, :, lanes],
                preferred_element_type=jnp.float32,
            )
            own = jnp.where(second, numerator[:, HD:], numerator[:, :HD])
            outs[prompt, pair] = (own / total).astype(jnp.bfloat16)
            level = top * factor + jnp.log(total)
            flat = jnp.transpose(jnp.broadcast_to(level, (wide_rows, HD)))
            stats[prompt, pair : pair + 1] = flat[:1]
        for target in range(dp_count * share):

            @pl.when(away(turn, target))
            def _():
                for copy in sends(turn, target):
                    copy.start()

        return carry

    lax.fori_loop(0, prompts, work, 0)

    first, _, pair, pairs, row, rows = region(rank, prompts, mp_count)
    start = pl.multiple_of(beam * beam_rows + row, 16)
    landed[me] = outs[pl.ds(first, each), pl.ds(pair, pairs), pl.ds(start, rows)]
    landed_stats[me] = stats[pl.ds(first, each)]

    def finish(delta, carry):
        peer = lax.rem(me + delta, count)
        for item in range(each):
            pltpu.make_async_remote_copy(
                src_ref=landed.at[me, item],
                dst_ref=landed.at[peer, item],
                send_sem=out_send.at[0, 0],
                recv_sem=out_recv.at[peer, item],
                device_id={"dp": peer // mp_count, "mp": lax.rem(peer, mp_count)},
                device_id_type=MESH,
            ).wait_recv()
            pltpu.make_async_remote_copy(
                src_ref=landed_stats.at[me, item],
                dst_ref=landed_stats.at[peer, item],
                send_sem=stat_send.at[0, 0],
                recv_sem=stat_recv.at[peer, item],
                device_id={"dp": peer // mp_count, "mp": lax.rem(peer, mp_count)},
                device_id_type=MESH,
            ).wait_recv()
        return carry

    lax.fori_loop(1, count, finish, 0)

    for item in range(each):
        levels = landed_stats[:, item]
        top = jnp.max(levels, axis=0, keepdims=True)
        shares = jnp.exp(levels - top)
        shares = shares / jnp.sum(shares, axis=0, keepdims=True)
        flipped[...] = jnp.transpose(shares.reshape(count * 8, shares.shape[-1]))
        columns = flipped[pl.ds(start, rows), :]
        for place in range(pairs):
            total = jnp.zeros((rows, HD), jnp.float32)
            for source in range(count):
                if pairs == 2:
                    column = columns[:, source * 8 + place : source * 8 + place + 1]
                else:
                    column = jnp.where(
                        pair == 1,
                        columns[:, source * 8 + 1 : source * 8 + 2],
                        columns[:, source * 8 : source * 8 + 1],
                    )
                total = total + column * landed[source, item, place].astype(jnp.float32)
            gathered[first + item, pair + place, pl.ds(pl.multiple_of(row, 16), rows)] = (
                total.astype(jnp.bfloat16)
            )

    def spread(delta):
        peer = lax.rem(rank + delta, mp_count)
        view = gathered.at[
            pl.ds(first, each), pl.ds(pair, pairs), pl.ds(pl.multiple_of(row, 16), rows)
        ]
        return pltpu.make_async_remote_copy(
            src_ref=view,
            dst_ref=view,
            send_sem=spread_send.at[delta],
            recv_sem=spread_recv.at[delta],
            device_id={"mp": peer},
            device_id_type=MESH,
        )

    for delta in range(1, mp_count):
        spread(delta).start()
    for delta in range(1, mp_count):
        spread(delta).wait()

    def drain(turn, carry):
        for target in range(dp_count * share):

            @pl.when(away(turn, target))
            def _():
                for copy in sends(turn, target):
                    copy.wait_send()

        return carry

    lax.fori_loop(0, prompts, drain, 0)
    out_ref[...] = gathered[...]


def attend(query, prompt_keys, prompt_values, extra_keys, extra_values, mask, dp_count, mp_count):
    prompts, pairs, rows, _ = query.shape
    count = dp_count * mp_count
    _, each, _, some_pairs, _, some_rows = region(0, prompts, mp_count)
    targets = dp_count * max(1, mp_count // prompts)
    vmem = pl.BlockSpec(memory_space=pltpu.VMEM)
    hbm = pl.BlockSpec(memory_space=pl.ANY)
    dma = pltpu.SemaphoreType.DMA
    merged = (prompts, pairs, rows // dp_count, HD)
    return pl.pallas_call(
        functools.partial(attend_kernel, dp_count, mp_count),
        out_shape=jax.ShapeDtypeStruct(merged, jnp.bfloat16),
        in_specs=[vmem, hbm, hbm, vmem, vmem, vmem],
        out_specs=vmem,
        scratch_shapes=[
            pltpu.VMEM((2,) + prompt_keys.shape[1:], jnp.bfloat16),
            pltpu.VMEM((2,) + prompt_values.shape[1:], jnp.bfloat16),
            pltpu.VMEM((prompts, pairs, rows, HD), jnp.bfloat16),
            pltpu.VMEM((prompts, 8, rows), jnp.float32),
            pltpu.VMEM((count, each, some_pairs, some_rows, HD), jnp.bfloat16),
            pltpu.VMEM((count, each, 8, rows), jnp.float32),
            pltpu.VMEM((rows, count * 8), jnp.float32),
            pltpu.VMEM(merged, jnp.bfloat16),
            dma((2,)),
            dma((2,)),
            dma((prompts, targets)),
            dma((count, each)),
            dma((prompts, targets)),
            dma((count, each)),
            dma((mp_count,)),
            dma((mp_count,)),
        ],
        compiler_params=pltpu.CompilerParams(
            collective_id=1, has_side_effects=True, vmem_limit_bytes=VMEM_LIMIT
        ),
        name="attend",
    )(query, prompt_keys, prompt_values, extra_keys, extra_values, mask)


def lineage(parents, step, stop):
    beams = parents.shape[2]
    source = jnp.broadcast_to(jnp.arange(beams, dtype=jnp.int32)[None, :], parents.shape[1:])
    for later in range(step, stop, -1):
        choice = source[:, :, None] == jnp.arange(beams, dtype=jnp.int32)
        source = jnp.sum(jnp.where(choice, parents[later][:, None, :], 0), axis=-1)
    return source


def on_device(
    hidden,
    gain,
    w_query,
    w_key,
    w_value,
    query_bias,
    key_bias,
    value_bias,
    w_out,
    prompt_keys,
    prompt_values,
    gen_keys,
    gen_values,
    parents,
):
    beam = lax.axis_index("dp")
    rank = lax.axis_index("mp")
    beams = lax.axis_size("dp")
    mp_count = lax.axis_size("mp")
    steps, prompts = hidden.shape[:2]
    rows = steps * prompts
    per_rank = QH // mp_count + 2

    widened = hidden.reshape(rows, -1).astype(jnp.float32)
    squares = jnp.sum(widened * widened, axis=-1, keepdims=True)
    scaled = (widened * gain).astype(jnp.bfloat16)
    places = QH // mp_count
    narrow = [min(owner, KVH - 1) for owner in range(mp_count)]
    narrow_bias = [
        jnp.stack([array[head * HD : (head + 1) * HD] for head in narrow])[:, None]
        for array in (key_bias, value_bias)
    ]
    bias = jnp.concatenate([query_bias.reshape(mp_count, places, HD)] + narrow_bias, axis=1)
    projected = exchange(
        scaled,
        w_query,
        w_key,
        w_value,
        jnp.broadcast_to(squares, (rows, HD)),
        bias.reshape(mp_count * per_rank, HD),
        beams,
        mp_count,
        per_rank,
    ).reshape(beams, mp_count, per_rank, rows, HD)

    query = projected[:, :, :places].reshape(beams, 2, 2, REPEAT, steps, prompts, HD)
    query = query.transpose(5, 1, 0, 2, 4, 3, 6)
    split = jnp.arange(2)
    same = (split[:, None] == split[None, :])[None, None, None, :, None, None, :, None]
    query = jnp.where(same, query[:, :, :, :, :, :, None, :], jnp.bfloat16(0))
    query = query.reshape(prompts, 2, beams * 2 * steps * REPEAT, 2 * HD)

    own = lax.dynamic_index_in_dim(projected, beam, 0, keepdims=False)
    fresh = own[:KVH, places:].reshape(KVH, 2, steps, prompts, HD).transpose(1, 3, 2, 0, 4)
    fresh = fresh.reshape(2, prompts, steps, KVH * HD)
    width = gen_keys.shape[2]
    extras = -(-(width + steps) // 16) * 16
    pad = jnp.zeros((prompts, extras - width - steps, KVH * HD), jnp.bfloat16)
    extra_keys = jnp.concatenate([gen_keys[:, 0], fresh[0], pad], axis=1)
    extra_values = jnp.concatenate([gen_values[:, 0], fresh[1], pad], axis=1)

    seen = []
    for step in range(steps):
        anchor = lineage(parents, step, -1) == beam
        columns = [jnp.broadcast_to(anchor[:, :, None], (prompts, beams, width))]
        for source in range(steps):
            if source <= step:
                flag = (lineage(parents, step, source) == beam) & (rank == 0)
            else:
                flag = jnp.zeros((prompts, beams), jnp.bool_)
            columns.append(flag[:, :, None])
        columns.append(jnp.zeros((prompts, beams, extras - width - steps), jnp.bool_))
        seen.append(jnp.concatenate(columns, axis=2))
    mask = jnp.where(jnp.stack(seen, axis=2), jnp.float32(0), jnp.float32(hidden_fill))
    mask = jnp.broadcast_to(
        mask[:, :, None, :, None, :], (prompts, beams, 2, steps, REPEAT, extras)
    ).reshape(prompts, beams * 2 * steps * REPEAT, extras)

    attended = attend(
        query, prompt_keys, prompt_values, extra_keys, extra_values, mask, beams, mp_count
    )
    attended = attended.reshape(prompts, 2, 2, steps, REPEAT, HD).transpose(3, 0, 1, 2, 4, 5)
    attended = attended.reshape(rows, QH * HD)
    result = jnp.dot(attended, w_out, preferred_element_type=jnp.float32).astype(jnp.bfloat16)
    return result.reshape(steps, prompts, 1, -1)


def solution(mesh):
    return jax.shard_map(
        on_device,
        mesh=mesh,
        in_specs=(
            P(None, "groups", "dp", "mp"),
            P("mp"),
            P("mp", None),
            P("mp", None),
            P("mp", None),
            P(),
            P(),
            P(),
            P(None, "mp"),
            P("groups", ("dp", "mp"), None),
            P("groups", ("dp", "mp"), None),
            P("groups", "dp", "mp", None),
            P("groups", "dp", "mp", None),
            P(None, "groups", None),
        ),
        out_specs=P(None, "groups", "dp", "mp"),
        check_vma=False,
    )
```
